256 devices in a mesh: pipe: 16 (over x, z_hi), tensor: 16 (over y, z_lo, core).
Axes of the slice: x: 4, y: 4, z: 8 (z_hi: 4, z_lo: 2; z = z_hi * 2 + z_lo), core: 2. Of those that a mesh axis runs over, the one named last changes fastest.
Arguments:
- section_weights: bfloat16 [16, 2, 4096, 4096], P('pipe', None, 'tensor'), may hold values from -0.09375 to 0.09375
- context: bfloat16 [16, 2, 768, 4096], P('pipe', None, None, 'tensor'), may hold values from -3 to 3
- grad_out: bfloat16 [16, 2, 768, 4096], P('pipe', None, 'tensor'), may hold values from -3 to 3
Outputs:
- weight_grad: bfloat16 [16, 4096, 4096], P('pipe', 'tensor')
- input_grad: bfloat16 [16, 2, 768, 4096], P('pipe', None, None, 'tensor')
The draws below stay inside these ranges and needn't reach their ends.
All inputs are finite; a program needn't handle non-finite values.
Results may differ from the reference program's by a relative error of at most 0.001.
Values may be sent and summed in bfloat16 or wider, within the bound.
No kernel may reach another device: no remote copies, remote signals or barrier semaphores. Data moves between devices by JAX's collectives and lax.ppermute only.
A program may use at most 128 MiB of HBM per device.

```python
import jax
import jax.numpy as jnp
from jax import lax

DI = 4096
DO = 4096
TOK = 768
SECTIONS = 16


def level_of(stream_key, shape, cuts, low, largest):
    def one(dim, shards_of):
        draws = jax.random.uniform(jax.random.fold_in(jax.random.fold_in(stream_key, 6), dim), (shards_of,), jnp.float32, low / len(cuts), largest / len(cuts))
        return jnp.repeat(jnp.exp(draws), shape[dim] // shards_of).reshape((-1,) + (1,) * (len(shape) - dim - 1))

    factor_of = one(*cuts[0])
    for cut in cuts[1:]:
        factor_of = factor_of * one(*cut)
    return factor_of


def noise(stream_key, dims, scale, limit, shards=(), kind=jnp.bfloat16):
    loudness = level_of(stream_key, dims, shards, -0.22, 0.18) if shards else 1.0
    entries = jax.random.normal(stream_key, dims, jnp.float32) * scale * loudness
    return jnp.minimum(jnp.maximum(entries, -limit), limit).astype(kind)


def setup_inputs(seed: int = 0) -> dict:
    streams_of = jax.random.split(jax.random.key(seed), 4)
    return {
        "section_weights": noise(streams_of[0], (SECTIONS, 2, DI, DO), DO ** -0.5, 0.09375, ((0, 16), (2, 16))),
        "context": noise(streams_of[1], (SECTIONS, 2, TOK, DI), 0.2, 3.0, ((0, 16), (3, 16))),
        "grad_out": noise(streams_of[2], (SECTIONS, 2, TOK, DO), 0.2, 3.0, ((0, 16), (2, 16))),
    }


def reference(section_weights, context, grad_out):
    sections = context.shape[0]

    def section_grad(position):
        mirror = sections - 1 - position
        down = jnp.dot(context[position, 0].T, grad_out[position, 0], preferred_element_type=jnp.float32)
        up = jnp.dot(context[mirror, 1].T, grad_out[mirror, 1], preferred_element_type=jnp.float32)
        return (down + up).astype(jnp.bfloat16)
    weight_grad = lax.map(section_grad, jnp.arange(sections, dtype=jnp.int32))

    def backward(position):
        first = jnp.dot(grad_out[position, 0], section_weights[position, 0].T, preferred_element_type=jnp.float32)
        second = jnp.dot(grad_out[position, 1], section_weights[position, 1].T, preferred_element_type=jnp.float32)
        return jnp.stack([first, second]).astype(jnp.bfloat16)
    local = lax.map(backward, jnp.arange(sections, dtype=jnp.int32))
    empty = jnp.zeros_like(local[:1, 0])
    down_recv = jnp.concatenate([local[1:, 0], empty], axis=0)
    up_recv = jnp.concatenate([empty, local[:-1, 1]], axis=0)
    input_grad = jnp.stack([down_recv, up_recv], axis=1)
    return (weight_grad, input_grad)
```

```python
import functools

import jax
import jax.numpy as jnp
from jax import lax
from jax.experimental import pallas as pl
from jax.experimental.pallas import tpu as pltpu
from jax.sharding import PartitionSpec as P

RING = 4
PLANES = 2
CORES = 2
KEYS = tuple(
    (dy, dz, dc) for dc in range(CORES) for dy in (0, -1, 1, 2) for dz in range(PLANES)
)


def place(y, plane, core):
    return (y * PLANES + plane) * CORES + core


def moved(value, step):
    pairs = []
    for y in range(RING):
        for plane in range(PLANES):
            for core in range(CORES):
                pairs.append((place(y, plane, core), place(*step(y, plane, core))))
    return lax.ppermute(value, "tensor", pairs)


def upward(value):
    return moved(value, lambda y, plane, core: ((y + 1) % RING, plane, core))


def downward(value):
    return moved(value, lambda y, plane, core: ((y - 1) % RING, plane, core))


def across(value):
    return moved(value, lambda y, plane, core: (y, 1 - plane, core))


def to_sibling(value):
    return moved(value, lambda y, plane, core: (y, plane, 1 - core))


def mirrored(value):
    count = lax.axis_size("pipe")
    return lax.ppermute(value, "pipe", [(i, count - 1 - i) for i in range(count)])


def from_behind(value, by):
    count = lax.axis_size("pipe")
    pairs = [(i, i + by) for i in range(count) if 0 <= i + by < count]
    return lax.ppermute(value, "pipe", pairs)


def gathered(own):
    held = {(0, 0): own, (0, 1): across(own)}
    for dz in range(PLANES):
        held[(-1, dz)] = upward(held[(0, dz)])
        held[(1, dz)] = downward(held[(0, dz)])
    held[(2, 0)] = upward(held[(-1, 0)])
    held[(2, 1)] = downward(held[(1, 1)])
    whole = {}
    for (dy, dz), value in held.items():
        whole[(dy, dz, 0)] = value
        whole[(dy, dz, 1)] = to_sibling(value)
    return [whole[key] for key in KEYS]


def block_of(t, key):
    dy, dz, dc = key
    core = t % CORES
    plane = (t // CORES) % PLANES
    y = t // (CORES * PLANES)
    if dc:
        core = 1 - core
    if dz:
        plane = 1 - plane
    return place((y + dy + RING) % RING, plane, core)


def loads(blocks, whole, sems):
    t = lax.axis_index("tensor")
    rows = blocks[0].shape[-2]
    copies = []
    for i, key in enumerate(KEYS):
        start = pl.multiple_of(block_of(t, key) * rows, rows)
        if len(whole.shape) == 3:
            target = whole.at[:, pl.ds(start, rows), :]
        else:
            target = whole.at[pl.ds(start, rows), :]
        copies.append(pltpu.make_async_copy(blocks[i], target, sems.at[i]))
    return copies


def first_kernel(*refs):
    n = len(KEYS)
    blocks = refs[:n]
    weights, context, back0, back1, total, whole, held, sems, wsem = refs[n:]
    copies = loads(blocks, whole, sems)
    wcopy = pltpu.make_async_copy(weights, held, wsem)
    wcopy.start()
    for copy in copies:
        copy.start()
    wcopy.wait()
    for copy in copies:
        copy.wait()
    tile = 256
    for r, out in enumerate((back0, back1)):
        @pl.loop(0, out.shape[0] // tile)
        def _(i, r=r, out=out):
            rows = pl.ds(pl.multiple_of(i * tile, tile), tile)
            out[rows, :] = lax.dot_general(
                whole[r, rows, :], held[r], (((1,), (1,)), ((), ())),
                preferred_element_type=jnp.float32,
            ).astype(out.dtype)
    wide = 512

    @pl.loop(0, total.shape[1] // wide)
    def _(i):
        cols = pl.ds(pl.multiple_of(i * wide, wide), wide)
        total[:, cols] = jnp.dot(
            context[...], whole[0, :, cols], preferred_element_type=jnp.float32
        )


def last_kernel(*refs):
    n = len(KEYS)
    blocks = refs[:n]
    context, total, out, whole, sems = refs[n:]
    copies = loads(blocks, whole, sems)
    for copy in copies:
        copy.start()
    for copy in copies:
        copy.wait()
    wide = 512

    @pl.loop(0, out.shape[1] // wide)
    def _(i):
        cols = pl.ds(pl.multiple_of(i * wide, wide), wide)
        out[:, cols] = (
            total[:, cols]
            + jnp.dot(context[...], whole[:, cols], preferred_element_type=jnp.float32)
        ).astype(out.dtype)


ANY = pl.BlockSpec(memory_space=pl.ANY)
VMEM = pl.BlockSpec(memory_space=pltpu.VMEM)


def shards(section_weights, context, grad_out):
    tokens, width_in = context.shape[2:]
    width_out = grad_out.shape[3]
    n = len(KEYS)
    both = grad_out[0]
    far = mirrored(both[1])
    far_context = mirrored(context[0, 1])
    near_blocks = gathered(both)
    far_blocks = gathered(far)
    params = pltpu.CompilerParams(vmem_limit_bytes=40 * 2**20)
    flops = 2 * tokens * width_in * width_out
    back0, back1, total = pl.pallas_call(
        first_kernel,
        out_shape=(
            jax.ShapeDtypeStruct((tokens, width_in), jnp.bfloat16),
            jax.ShapeDtypeStruct((tokens, width_in), jnp.bfloat16),
            jax.ShapeDtypeStruct((width_in, width_out), jnp.float32),
        ),
        in_specs=[ANY] * n + [ANY, VMEM],
        out_specs=(VMEM, VMEM, VMEM),
        scratch_shapes=[
            pltpu.VMEM((2, tokens, width_out), jnp.bfloat16),
            pltpu.VMEM((2, width_in, width_out), jnp.bfloat16),
            pltpu.SemaphoreType.DMA((n,)),
            pltpu.SemaphoreType.DMA,
        ],
        compiler_params=params,
        cost_estimate=pl.CostEstimate(
            flops=3 * flops, bytes_accessed=2 * (2 * tokens + 4 * width_in) * width_out,
            transcendentals=0,
        ),
    )(*near_blocks, section_weights[0], context[0, 0].T)
    weight_grad = pl.pallas_call(
        last_kernel,
        out_shape=jax.ShapeDtypeStruct((width_in, width_out), jnp.bfloat16),
        in_specs=[ANY] * n + [VMEM, VMEM],
        out_specs=VMEM,
        scratch_shapes=[
            pltpu.VMEM((tokens, width_out), jnp.bfloat16),
            pltpu.SemaphoreType.DMA((n,)),
        ],
        compiler_params=params,
        cost_estimate=pl.CostEstimate(
            flops=flops, bytes_accessed=2 * (tokens + 3 * width_in) * width_out,
            transcendentals=0,
        ),
    )(*far_blocks, far_context.T, total)
    from_next = from_behind(back0, -1)
    from_prior = from_behind(back1, 1)
    input_grad = jnp.stack([from_next, from_prior])[None]
    return (weight_grad[None], input_grad)


def solution(mesh):
    placed = (
        P("pipe", None, "tensor", None),
        P("pipe", None, None, "tensor"),
        P("pipe", None, "tensor", None),
    )
    return jax.shard_map(
        shards,
        mesh=mesh,
        in_specs=placed,
        out_specs=(P("pipe", "tensor", None), P("pipe", None, None, "tensor")),
        check_vma=False,
    )
```

```python
import jax
import jax.numpy as jnp
from jax import lax
from jax.experimental import pallas as pl
from jax.experimental.pallas import tpu as pltpu
from jax.sharding import PartitionSpec as P

RING = 4
PLANES = 2
CORES = 2
HOPS = range(RING)
NEAR = tuple((hop, dz, 0) for dz in range(PLANES) for hop in HOPS)
EARLY = tuple((hop, dz, 0) for dz in range(PLANES) for hop in (0, 1))
LATE = tuple((hop, dz, dc) for hop in (2, 3) for dz in range(PLANES) for dc in range(CORES))
ANY = pl.BlockSpec(memory_space=pl.ANY)
VMEM = pl.BlockSpec(memory_space=pltpu.VMEM)


def place(y, plane, core):
    return (y * PLANES + plane) * CORES + core


def moved(value, step):
    pairs = []
    for y in range(RING):
        for plane in range(PLANES):
            for core in range(CORES):
                pairs.append((place(y, plane, core), place(*step(y, plane, core))))
    return lax.ppermute(value, "tensor", pairs)


def around(value):
    return moved(value, lambda y, plane, core: ((y + 1 - 2 * core) % RING, plane, core))


def across(value):
    return moved(value, lambda y, plane, core: (y, 1 - plane, core))


def to_sibling(value):
    return moved(value, lambda y, plane, core: (y, plane, 1 - core))


def mirrored(value):
    count = lax.axis_size("pipe")
    return lax.ppermute(value, "pipe", [(i, count - 1 - i) for i in range(count)])


def from_behind(value, by, other):
    count, group = lax.axis_size("pipe"), lax.axis_size("tensor")
    pairs = []
    for i in range(count):
        if 0 <= i + by < count:
            for t in range(group):
                target = t + 1 - 2 * (t % CORES) if other else t
                pairs.append((i * group + t, (i + by) * group + target))
    return lax.ppermute(value, ("pipe", "tensor"), pairs)


def after(value, *earlier):
    return lax.optimization_barrier((value, *earlier))[0]


def origin(key):
    t = lax.axis_index("tensor")
    hop, dz, dc = key
    core = t % CORES
    plane = (t // CORES) % PLANES
    y = t // (CORES * PLANES)
    if dc:
        core = 1 - core
    if dz:
        plane = 1 - plane
    y = (y + RING - hop + 2 * hop * core) % RING
    return y, plane, core


def back_kernel(*refs):
    n = len(NEAR)
    blocks = refs[:n], refs[n : 2 * n]
    own_w, sib_w, own0, own1, sib0, sib1, whole, held, bsems, wsems = refs[2 * n :]
    rows = blocks[0][0].shape[0]
    copies = []
    for r in range(2):
        copies.append(pltpu.make_async_copy(own_w.at[r], held.at[r, 0], wsems.at[r, 0]))
        copies.append(pltpu.make_async_copy(sib_w.at[r], held.at[r, 1], wsems.at[r, 1]))
    for i, key in enumerate(NEAR):
        y, plane, _ = origin(key)
        start = pl.multiple_of((y * PLANES + plane) * rows, rows)
        for r in range(2):
            copies.append(
                pltpu.make_async_copy(
                    blocks[r][i], whole.at[r, pl.ds(start, rows), :], bsems.at[r, i]
                )
            )
    for copy in copies:
        copy.start()
    for copy in copies:
        copy.wait()
    for r, outs in enumerate(((own0, sib0), (own1, sib1))):
        for which, out in enumerate(outs):
            out[...] = lax.dot_general(
                whole[r], held[r, which], (((1,), (1,)), ((), ())),
                preferred_element_type=jnp.float32,
            ).astype(out.dtype)


def sum_kernel(*refs):
    n, m = len(NEAR), len(EARLY)
    near, far = refs[:n], refs[n : n + m]
    near_own, near_sib, far_own, far_sib, own, sib, whole, upright, flat, bsems, csems = refs[n + m :]
    rows = far[0].shape[0]
    width = near_own.shape[1]
    copies = []
    for i, block in enumerate(near + far):
        copies.append(
            pltpu.make_async_copy(block, whole.at[pl.ds(i * rows, rows), :], bsems.at[i])
        )
    for j, (a, b) in enumerate(((near_own, far_own), (near_sib, far_sib))):
        for i, key in enumerate(NEAR + EARLY):
            start = pl.multiple_of(place(*origin(key)) * rows, rows)
            source = a if i < n else b
            copies.append(
                pltpu.make_async_copy(
                    source.at[pl.ds(start, rows), :],
                    upright.at[j, pl.ds(i * rows, rows), :],
                    csems.at[j, i],
                )
            )
    for copy in copies:
        copy.start()
    for copy in copies:
        copy.wait()
    wide = 512
    for j, out in ((1, sib), (0, own)):
        flat[...] = upright[j].T

        @pl.loop(0, out.shape[1] // wide)
        def _(i, out=out):
            cols = pl.ds(pl.multiple_of(i * wide, wide), wide)
            out[:, cols] = jnp.dot(
                flat[...], whole[:, cols], preferred_element_type=jnp.float32
            )


def last_kernel(*refs):
    n = len(LATE)
    blocks = refs[:n]
    context, mine, theirs, out, whole, upright, flat, bsems, csems = refs[n:]
    rows = blocks[0].shape[0]
    copies = []
    for i, key in enumerate(LATE):
        start = pl.multiple_of(place(*origin(key)) * rows, rows)
        copies.append(
            pltpu.make_async_copy(
                context.at[pl.ds(start, rows), :],
                upright.at[pl.ds(i * rows, rows), :],
                csems.at[i],
            )
        )
        copies.append(
            pltpu.make_async_copy(blocks[i], whole.at[pl.ds(i * rows, rows), :], bsems.at[i])
        )
    for copy in copies:
        copy.start()
    for copy in copies:
        copy.wait()
    flat[...] = upright[...].T
    wide = 512

    @pl.loop(0, out.shape[1] // wide)
    def _(i):
        cols = pl.ds(pl.multiple_of(i * wide, wide), wide)
        out[:, cols] = (
            mine[:, cols]
            + theirs[:, cols]
            + jnp.dot(flat[...], whole[:, cols], preferred_element_type=jnp.float32)
        ).astype(out.dtype)


def interleaved(same, other):
    core = lax.axis_index("tensor") % CORES
    a = same.reshape(RING * PLANES, -1, same.shape[1])
    b = other.reshape(RING * PLANES, -1, same.shape[1])
    even = jnp.where(core == 0, a, b)
    odd = jnp.where(core == 0, b, a)
    return jnp.stack([even, odd], axis=1).reshape(-1, same.shape[1])


def shards(section_weights, context, grad_out):
    width_in = context.shape[3]
    rows, width_out = grad_out.shape[2:]
    own_w = section_weights[0]
    near_own = context[0, 0]
    held = {("A", 0, 0): grad_out[0, 0], ("B", 0, 0): grad_out[0, 1]}
    held["M", 0, 0] = mirrored(held["B", 0, 0])
    for name in "AB":
        held[name, 0, 1] = across(held[name, 0, 0])
    sib_w = to_sibling(own_w)
    near_sib = to_sibling(near_own)
    far_own = mirrored(context[0, 1])
    order = [(name, hop, dz) for dz in range(PLANES) for hop in HOPS[1:] for name in "AB"]
    order += [("M", hop, dz) for hop in HOPS[1:] for dz in range(PLANES)]
    waits = {
        ("B", 3, 0): ("A", 0, 1),
        ("A", 1, 1): ("B", 0, 1),
        ("A", 2, 1): ("M", 0, 0),
        ("B", 3, 1): ("M", 0, 1),
    }
    for i, key in enumerate(order):
        name, hop, dz = key
        earlier = [held[order[i - 2]]] if i > 1 else []
        if key in waits:
            earlier.append(held[waits[key]])
        if key == ("M", 1, 0):
            earlier.append(far_own)
        held[key] = around(after(held[name, hop - 1, dz], *earlier))
        if key == ("A", 2, 1):
            held["M", 0, 1] = across(held["M", 0, 0])
        if key == ("M", 1, 0):
            far_sib = to_sibling(far_own)

    half = RING * PLANES * rows
    back_shape = jax.ShapeDtypeStruct((half, width_in), jnp.bfloat16)
    own0, own1, sib0, sib1 = pl.pallas_call(
        back_kernel,
        out_shape=(back_shape,) * 4,
        in_specs=[ANY] * (2 * len(NEAR) + 2),
        out_specs=(VMEM,) * 4,
        scratch_shapes=[
            pltpu.VMEM((2, half, width_out), jnp.bfloat16),
            pltpu.VMEM((2, 2, width_in, width_out), jnp.bfloat16),
            pltpu.SemaphoreType.DMA((2, len(NEAR))),
            pltpu.SemaphoreType.DMA((2, 2)),
        ],
        compiler_params=pltpu.CompilerParams(vmem_limit_bytes=24 * 2**20),
        cost_estimate=pl.CostEstimate(
            flops=8 * half * width_in * width_out,
            bytes_accessed=4 * (half + 2 * width_in) * width_out,
            transcendentals=0,
        ),
    )(*(held[name, *key[:2]] for name in "AB" for key in NEAR), own_w, sib_w)

    sum_shape = jax.ShapeDtypeStruct((width_in, width_out), jnp.float32)
    count = len(NEAR) + len(EARLY)
    mine, for_sibling = pl.pallas_call(
        sum_kernel,
        out_shape=(sum_shape,) * 2,
        in_specs=[ANY] * (count + 4),
        out_specs=(VMEM,) * 2,
        scratch_shapes=[
            pltpu.VMEM((count * rows, width_out), jnp.bfloat16),
            pltpu.VMEM((2, count * rows, width_in), jnp.bfloat16),
            pltpu.VMEM((width_in, count * rows), jnp.bfloat16),
            pltpu.SemaphoreType.DMA((count,)),
            pltpu.SemaphoreType.DMA((2, count)),
        ],
        compiler_params=pltpu.CompilerParams(vmem_limit_bytes=24 * 2**20),
        cost_estimate=pl.CostEstimate(
            flops=4 * count * rows * width_in * width_out,
            bytes_accessed=(2 * count * rows + 8 * width_in) * width_out,
            transcendentals=0,
        ),
    )(
        *(held["A", *key[:2]] for key in NEAR),
        *(held["M", *key[:2]] for key in EARLY),
        near_own, near_sib, far_own, after(far_sib, own0),
    )
    theirs = to_sibling(for_sibling)

    late = []
    for key in LATE:
        value = held["M", *key[:2]]
        late.append(to_sibling(value) if key[2] else value)
    count = len(LATE)
    weight_grad = pl.pallas_call(
        last_kernel,
        out_shape=jax.ShapeDtypeStruct((width_in, width_out), jnp.bfloat16),
        in_specs=[ANY] * (count + 1) + [VMEM, VMEM],
        out_specs=VMEM,
        scratch_shapes=[
            pltpu.VMEM((count * rows, width_out), jnp.bfloat16),
            pltpu.VMEM((count * rows, width_in), jnp.bfloat16),
            pltpu.VMEM((width_in, count * rows), jnp.bfloat16),
            pltpu.SemaphoreType.DMA((count,)),
            pltpu.SemaphoreType.DMA((count,)),
        ],
        compiler_params=pltpu.CompilerParams(vmem_limit_bytes=24 * 2**20),
        cost_estimate=pl.CostEstimate(
            flops=2 * count * rows * width_in * width_out,
            bytes_accessed=(2 * count * rows + 10 * width_in) * width_out,
            transcendentals=0,
        ),
    )(*late, far_own, mine, theirs)

    from_next = interleaved(from_behind(own0, -1, False), from_behind(sib0, -1, True))
    from_prior = interleaved(from_behind(own1, 1, False), from_behind(sib1, 1, True))
    input_grad = jnp.stack([from_next, from_prior])[None]
    return (weight_grad[None], input_grad)


def solution(mesh):
    placed = (
        P("pipe", None, "tensor", None),
        P("pipe", None, None, "tensor"),
        P("pipe", None, "tensor", None),
    )
    return jax.shard_map(
        shards,
        mesh=mesh,
        in_specs=placed,
        out_specs=(P("pipe", "tensor", None), P("pipe", None, None, "tensor")),
        check_vma=False,
    )
```

```python
import functools

import jax
import jax.numpy as jnp
from jax import lax
from jax.experimental import pallas as pl
from jax.experimental.pallas import tpu as pltpu
from jax.sharding import PartitionSpec as P

RING = 4
PLANES = 2
CORES = 2
ANY = pl.BlockSpec(memory_space=pl.ANY)
VMEM = pl.BlockSpec(memory_space=pltpu.VMEM)
HBM = pl.BlockSpec(memory_space=pltpu.HBM)
NEAR = tuple((dy, dz, dc) for dz in range(PLANES) for dy in (0, -1, 1, 2) for dc in range(CORES))
LATE = tuple((2, dz, dc) for dz in range(PLANES) for dc in range(CORES))
EARLY = tuple(key for key in NEAR if key not in LATE)


def place(y, plane, core):
    return (y * PLANES + plane) * CORES + core


def moved(value, step):
    pairs = []
    for y in range(RING):
        for plane in range(PLANES):
            for core in range(CORES):
                pairs.append((place(y, plane, core), place(*step(y, plane, core))))
    return lax.ppermute(value, "tensor", pairs)


def upward(value):
    return moved(value, lambda y, plane, core: ((y + 1) % RING, plane, core))


def downward(value):
    return moved(value, lambda y, plane, core: ((y - 1) % RING, plane, core))


def across(value):
    return moved(value, lambda y, plane, core: (y, 1 - plane, core))


def to_sibling(value):
    return moved(value, lambda y, plane, core: (y, plane, 1 - core))


def mirrored(value):
    count = lax.axis_size("pipe")
    return lax.ppermute(value, "pipe", [(i, count - 1 - i) for i in range(count)])


def from_behind(value, by):
    count = lax.axis_size("pipe")
    pairs = [(i, i + by) for i in range(count) if 0 <= i + by < count]
    return lax.ppermute(value, "pipe", pairs)


def after(value, *earlier):
    return lax.optimization_barrier((value, *earlier))[0]


def first_row(key, rows):
    t = lax.axis_index("tensor")
    dy, dz, dc = key
    core = t % CORES
    plane = (t // CORES) % PLANES
    y = (t // (CORES * PLANES) + dy + RING) % RING
    block = place(y, 1 - plane if dz else plane, 1 - core if dc else core)
    return pl.multiple_of(block * rows, rows)


def run(copies):
    for copy in copies:
        copy.start()
    for copy in copies:
        copy.wait()


def back_kernel(*refs):
    n = len(NEAR)
    blocks = refs[:n]
    weights, first, second, whole, held, bsems, wsems = refs[n:]
    rows = blocks[0].shape[1]
    copies = [pltpu.make_async_copy(weights.at[r], held.at[r], wsems.at[r]) for r in range(2)]
    for i, key in enumerate(NEAR):
        target = whole.at[:, pl.ds(first_row(key, rows), rows), :]
        copies.append(pltpu.make_async_copy(blocks[i], target, bsems.at[i]))
    run(copies)
    tile = 384
    for r, out in enumerate((first, second)):
        for i in range(out.shape[0] // tile):
            span = slice(i * tile, (i + 1) * tile)
            out[span, :] = lax.dot_general(
                whole[r, span, :], held[r], (((1,), (1,)), ((), ())),
                preferred_element_type=jnp.float32,
            ).astype(out.dtype)


def sum_kernel(keys, late_keys, more, *refs):
    n = len(keys)
    blocks, context, rest = refs[:n], refs[n], refs[n + 1 :]
    if more:
        before, *rest = rest
    if late_keys:
        total, late, *rest = rest
    else:
        total, *rest = rest
    whole, upright, flat, bsems, csems = rest
    rows = whole.shape[0] // n
    copies = []
    for i, block in enumerate(blocks):
        source = block.at[0] if len(block.shape) == 3 else block
        copies.append(
            pltpu.make_async_copy(source, whole.at[pl.ds(i * rows, rows), :], bsems.at[i])
        )
    for i, key in enumerate(keys + late_keys):
        source = context.at[pl.ds(first_row(key, rows), rows), :]
        target = upright.at[pl.ds(i * rows, rows), :]
        copies.append(pltpu.make_async_copy(source, target, csems.at[i]))
    run(copies)
    count = n * rows
    flat[...] = upright[pl.ds(0, count), :].T
    if late_keys:
        late[...] = upright[pl.ds(count, len(late_keys) * rows), :].T
    wide = 512

    @pl.loop(0, total.shape[1] // wide)
    def _(i):
        cols = pl.ds(pl.multiple_of(i * wide, wide), wide)
        product = jnp.dot(flat[...], whole[:, cols], preferred_element_type=jnp.float32)
        total[:, cols] = before[:, cols] + product if more else product


def last_kernel(*refs):
    n = len(LATE)
    context, total, out, whole = refs[n:]
    rows = refs[0].shape[0]
    for i, block in enumerate(refs[:n]):
        whole[pl.ds(i * rows, rows), :] = block[...]
    out[...] = (
        total[...] + jnp.dot(context[...], whole[...], preferred_element_type=jnp.float32)
    ).astype(out.dtype)


def shards(section_weights, context, grad_out):
    tokens, width_in = context.shape[2:]
    rows, width_out = grad_out.shape[2:]
    flops = 2 * tokens * width_in * width_out

    near = {(0, 0, 0): grad_out[0]}
    far = {}

    def send(held, move, begin, end, *earlier):
        key = (*end, int(move is to_sibling))
        held[key] = move(after(held[(*begin, 0)], *earlier))
        return held[key]

    def share(held, *spots):
        for spot in spots:
            held[(*spot, 1)] = to_sibling(held[(*spot, 0)])
        return [held[(*spot, 1)] for spot in spots]

    step = [
        send(near, upward, (0, 0), (-1, 0)),
        send(near, downward, (0, 0), (1, 0)),
        send(near, across, (0, 0), (0, 1)),
    ]
    far[0, 0, 0] = mirrored(after(grad_out[0, 1], *step))
    up_context = context[0, 1]
    step.append(up_context)
    step = [
        send(near, upward, (-1, 0), (2, 0), *step),
        send(near, downward, (0, 1), (1, 1), *step),
        far[0, 0, 0],
        *share(near, (0, 0), (-1, 0), (1, 0), (0, 1)),
    ]
    far_context = mirrored(after(up_context, *step))
    step = [
        send(near, upward, (0, 1), (-1, 1), *step),
        send(near, downward, (1, 1), (2, 1), *step),
        send(far, across, (0, 0), (0, 1), *step),
        far_context,
    ]
    for spot in ((2, 0), (1, 1)):
        send(near, to_sibling, spot, spot, far[0, 1, 0])
    for spot in ((-1, 1), (2, 1)):
        send(near, to_sibling, spot, spot, *step)
    send(far, upward, (0, 0), (-1, 0), *step)
    send(far, downward, (0, 0), (1, 0), *step)

    back_shape = jax.ShapeDtypeStruct((tokens, width_in), jnp.bfloat16)
    back = pl.pallas_call(
        back_kernel,
        out_shape=(back_shape,) * 2,
        in_specs=[HBM] + [ANY] * (len(NEAR) - 1) + [HBM],
        out_specs=(VMEM,) * 2,
        scratch_shapes=[
            pltpu.VMEM((2, tokens, width_out), jnp.bfloat16),
            pltpu.VMEM((2, width_in, width_out), jnp.bfloat16),
            pltpu.SemaphoreType.DMA((len(NEAR),)),
            pltpu.SemaphoreType.DMA((2,)),
        ],
        compiler_params=pltpu.CompilerParams(vmem_limit_bytes=20 * 2**20),
        cost_estimate=pl.CostEstimate(
            flops=2 * flops, bytes_accessed=4 * (tokens + width_in) * width_out, transcendentals=0
        ),
    )(*(near[key] for key in NEAR), section_weights[0])
    from_next = from_behind(back[0], -1)
    from_prior = from_behind(back[1], 1)
    input_grad = jnp.stack([from_next, from_prior])[None]

    send(far, upward, (0, 1), (-1, 1), back[0])
    send(far, downward, (0, 1), (1, 1), back[0])
    send(far, upward, (-1, 0), (2, 0), back[0])

    def summed(keys, blocks, held, total, late):
        count = len(keys)
        everything = keys + late
        sizes = count * rows, len(late) * rows
        shapes = [jax.ShapeDtypeStruct((width_in, width_out), jnp.float32)]
        if late:
            shapes.append(jax.ShapeDtypeStruct((width_in, sizes[1]), jnp.bfloat16))
        return pl.pallas_call(
            functools.partial(sum_kernel, keys, late, total is not None),
            out_shape=tuple(shapes),
            in_specs=[ANY] * count + [ANY] + [VMEM] * (total is not None),
            out_specs=(VMEM,) * len(shapes),
            scratch_shapes=[
                pltpu.VMEM((sizes[0], width_out), jnp.bfloat16),
                pltpu.VMEM((sum(sizes), width_in), jnp.bfloat16),
                pltpu.VMEM((width_in, sizes[0]), jnp.bfloat16),
                pltpu.SemaphoreType.DMA((count,)),
                pltpu.SemaphoreType.DMA((len(everything),)),
            ],
            compiler_params=pltpu.CompilerParams(vmem_limit_bytes=18 * 2**20),
            cost_estimate=pl.CostEstimate(
                flops=2 * sizes[0] * width_in * width_out,
                bytes_accessed=(2 * sizes[0] + 6 * width_in) * width_out,
                transcendentals=0,
            ),
        )(*blocks, held, *([] if total is None else [total]))

    (total,) = summed(NEAR, [near[key] for key in NEAR], after(context[0, 0], *back), None, ())
    send(far, downward, (1, 1), (2, 1), total)
    for spot in ((0, 0), (0, 1), (-1, 0), (1, 0)):
        send(far, to_sibling, spot, spot, total)
    share(far, (-1, 1), (1, 1), (2, 0))
    send(far, to_sibling, (2, 1), (2, 1), from_next, from_prior)
    total, late_context = summed(EARLY, [far[key] for key in EARLY], far_context, total, LATE)
    late = len(LATE) * rows

    wide = 1024
    columns = pl.BlockSpec((width_in, wide), lambda i: (0, i))
    weight_grad = pl.pallas_call(
        last_kernel,
        out_shape=jax.ShapeDtypeStruct((width_in, width_out), jnp.bfloat16),
        grid=(width_out // wide,),
        in_specs=[pl.BlockSpec((rows, wide), lambda i: (0, i))] * len(LATE)
        + [pl.BlockSpec((width_in, late), lambda i: (0, 0)), columns],
        out_specs=columns,
        scratch_shapes=[pltpu.VMEM((late, wide), jnp.bfloat16)],
        compiler_params=pltpu.CompilerParams(vmem_limit_bytes=12 * 2**20),
        cost_estimate=pl.CostEstimate(
            flops=flops // 4, bytes_accessed=(2 * late + 6 * width_in) * width_out,
            transcendentals=0,
        ),
    )(*(far[key] for key in LATE), late_context, total)
    return (weight_grad[None], input_grad)


def solution(mesh):
    placed = (
        P("pipe", None, "tensor", None),
        P("pipe", None, None, "tensor"),
        P("pipe", None, "tensor", None),
    )
    return jax.shard_map(
        shards,
        mesh=mesh,
        in_specs=placed,
        out_specs=(P("pipe", "tensor", None), P("pipe", None, None, "tensor")),
        check_vma=False,
    )
```

```python
import functools

import jax
import jax.numpy as jnp
from jax import lax
from jax.experimental import pallas as pl
from jax.experimental.pallas import tpu as pltpu
from jax.sharding import PartitionSpec as P

RING = 4
PLANES = 2
CORES = 2
ANY = pl.BlockSpec(memory_space=pl.ANY)
VMEM = pl.BlockSpec(memory_space=pltpu.VMEM)
HBM = pl.BlockSpec(memory_space=pltpu.HBM)
NEAR = tuple((dy, dz, dc) for dz in range(PLANES) for dy in (0, -1, 1, 2) for dc in range(CORES))
LATE = tuple((2, dz, dc) for dz in range(PLANES) for dc in range(CORES))
EARLY = tuple(key for key in NEAR if key not in LATE)


def place(y, plane, core):
    return (y * PLANES + plane) * CORES + core


def moved(value, step):
    pairs = []
    for y in range(RING):
        for plane in range(PLANES):
            for core in range(CORES):
                pairs.append((place(y, plane, core), place(*step(y, plane, core))))
    return lax.ppermute(value, "tensor", pairs)


def upward(value):
    return moved(value, lambda y, plane, core: ((y + 1) % RING, plane, core))


def downward(value):
    return moved(value, lambda y, plane, core: ((y - 1) % RING, plane, core))


def across(value):
    return moved(value, lambda y, plane, core: (y, 1 - plane, core))


def to_sibling(value):
    return moved(value, lambda y, plane, core: (y, plane, 1 - core))


def mirrored(value):
    count = lax.axis_size("pipe")
    return lax.ppermute(value, "pipe", [(i, count - 1 - i) for i in range(count)])


def from_behind(value, by):
    count = lax.axis_size("pipe")
    pairs = [(i, i + by) for i in range(count) if 0 <= i + by < count]
    return lax.ppermute(value, "pipe", pairs)


def after(value, *earlier):
    return lax.optimization_barrier((value, *earlier))[0]


def first_row(key, rows):
    t = lax.axis_index("tensor")
    dy, dz, dc = key
    core = t % CORES
    plane = (t // CORES) % PLANES
    y = (t // (CORES * PLANES) + dy + RING) % RING
    block = place(y, 1 - plane if dz else plane, 1 - core if dc else core)
    return pl.multiple_of(block * rows, rows)


def run(copies):
    for copy in copies:
        copy.start()
    for copy in copies:
        copy.wait()


def back_kernel(*refs):
    n = len(NEAR)
    blocks = refs[:n]
    weights, first, second, whole, held, bsems, wsems = refs[n:]
    rows = blocks[0].shape[1]
    copies = [pltpu.make_async_copy(weights.at[r], held.at[r], wsems.at[r]) for r in range(2)]
    for i, key in enumerate(NEAR):
        target = whole.at[:, pl.ds(first_row(key, rows), rows), :]
        copies.append(pltpu.make_async_copy(blocks[i], target, bsems.at[i]))
    run(copies)
    tile = 384
    for r, out in enumerate((first, second)):
        for i in range(out.shape[0] // tile):
            span = slice(i * tile, (i + 1) * tile)
            out[span, :] = lax.dot_general(
                whole[r, span, :], held[r], (((1,), (1,)), ((), ())),
                preferred_element_type=jnp.float32,
            ).astype(out.dtype)


def sum_kernel(keys, late_keys, more, *refs):
    n = len(keys)
    blocks, context, rest = refs[:n], refs[n], refs[n + 1 :]
    if more:
        before, *rest = rest
    if late_keys:
        total, late, *rest = rest
    else:
        total, *rest = rest
    whole, upright, flat, bsems, csems = rest
    rows = whole.shape[0] // n
    copies = []
    for i, block in enumerate(blocks):
        source = block.at[0] if len(block.shape) == 3 else block
        copies.append(
            pltpu.make_async_copy(source, whole.at[pl.ds(i * rows, rows), :], bsems.at[i])
        )
    for i, key in enumerate(keys + late_keys):
        source = context.at[pl.ds(first_row(key, rows), rows), :]
        target = upright.at[pl.ds(i * rows, rows), :]
        copies.append(pltpu.make_async_copy(source, target, csems.at[i]))
    run(copies)
    count = n * rows
    flat[...] = upright[pl.ds(0, count), :].T
    if late_keys:
        late[...] = upright[pl.ds(count, len(late_keys) * rows), :].T
    wide = 512

    @pl.loop(0, total.shape[1] // wide)
    def _(i):
        cols = pl.ds(pl.multiple_of(i * wide, wide), wide)
        product = jnp.dot(flat[...], whole[:, cols], preferred_element_type=jnp.float32)
        total[:, cols] = before[:, cols] + product if more else product


def last_kernel(*refs):
    n = len(LATE)
    context, total, out, whole = refs[n:]
    rows = refs[0].shape[0]
    for i, block in enumerate(refs[:n]):
        whole[pl.ds(i * rows, rows), :] = block[...]
    out[...] = (
        total[...] + jnp.dot(context[...], whole[...], preferred_element_type=jnp.float32)
    ).astype(out.dtype)


def shards(section_weights, context, grad_out):
    tokens, width_in = context.shape[2:]
    rows, width_out = grad_out.shape[2:]
    flops = 2 * tokens * width_in * width_out

    near = {(0, 0, 0): grad_out[0]}
    far = {}

    def send(held, move, begin, end, *earlier):
        key = (*end, int(move is to_sibling))
        held[key] = move(after(held[(*begin, 0)], *earlier))
        return held[key]

    def share(held, *spots):
        for spot in spots:
            held[(*spot, 1)] = to_sibling(held[(*spot, 0)])
        return [held[(*spot, 1)] for spot in spots]

    step = [
        send(near, upward, (0, 0), (-1, 0)),
        send(near, downward, (0, 0), (1, 0)),
        send(near, across, (0, 0), (0, 1)),
    ]
    far[0, 0, 0] = mirrored(after(grad_out[0, 1], *step))
    up_context = context[0, 1]
    step.append(up_context)
    step = [
        send(near, upward, (-1, 0), (2, 0), *step),
        send(near, downward, (0, 1), (1, 1), *step),
        far[0, 0, 0],
        *share(near, (0, 0), (-1, 0), (1, 0), (0, 1)),
    ]
    step = [
        send(near, upward, (0, 1), (-1, 1), *step),
        send(near, downward, (1, 1), (2, 1), *step),
        send(far, across, (0, 0), (0, 1), *step),
    ]
    for spot in ((2, 0), (1, 1)):
        send(near, to_sibling, spot, spot, far[0, 1, 0])
    for spot in ((-1, 1), (2, 1)):
        send(near, to_sibling, spot, spot, *step)
    send(far, upward, (0, 0), (-1, 0), *step)
    send(far, downward, (0, 0), (1, 0), *step)
    far_context = mirrored(after(up_context, *step))

    back_shape = jax.ShapeDtypeStruct((tokens, width_in), jnp.bfloat16)
    back = pl.pallas_call(
        back_kernel,
        out_shape=(back_shape,) * 2,
        in_specs=[HBM] + [ANY] * (len(NEAR) - 1) + [HBM],
        out_specs=(VMEM,) * 2,
        scratch_shapes=[
            pltpu.VMEM((2, tokens, width_out), jnp.bfloat16),
            pltpu.VMEM((2, width_in, width_out), jnp.bfloat16),
            pltpu.SemaphoreType.DMA((len(NEAR),)),
            pltpu.SemaphoreType.DMA((2,)),
        ],
        compiler_params=pltpu.CompilerParams(vmem_limit_bytes=40 * 2**20),
        cost_estimate=pl.CostEstimate(
            flops=2 * flops, bytes_accessed=4 * (tokens + width_in) * width_out, transcendentals=0
        ),
    )(*(near[key] for key in NEAR), section_weights[0])
    from_next = from_behind(back[0], -1)
    from_prior = from_behind(back[1], 1)
    input_grad = jnp.stack([from_next, from_prior])[None]

    send(far, upward, (0, 1), (-1, 1), back[0])
    send(far, downward, (0, 1), (1, 1), back[0])
    send(far, upward, (-1, 0), (2, 0), back[0])

    def summed(keys, blocks, held, total, late):
        count = len(keys)
        everything = keys + late
        sizes = count * rows, len(late) * rows
        shapes = [jax.ShapeDtypeStruct((width_in, width_out), jnp.float32)]
        if late:
            shapes.append(jax.ShapeDtypeStruct((width_in, sizes[1]), jnp.bfloat16))
        return pl.pallas_call(
            functools.partial(sum_kernel, keys, late, total is not None),
            out_shape=tuple(shapes),
            in_specs=[ANY] * count + [ANY] + [VMEM] * (total is not None),
            out_specs=(VMEM,) * len(shapes),
            scratch_shapes=[
                pltpu.VMEM((sizes[0], width_out), jnp.bfloat16),
                pltpu.VMEM((sum(sizes), width_in), jnp.bfloat16),
                pltpu.VMEM((width_in, sizes[0]), jnp.bfloat16),
                pltpu.SemaphoreType.DMA((count,)),
                pltpu.SemaphoreType.DMA((len(everything),)),
            ],
            compiler_params=pltpu.CompilerParams(vmem_limit_bytes=18 * 2**20),
            cost_estimate=pl.CostEstimate(
                flops=2 * sizes[0] * width_in * width_out,
                bytes_accessed=(2 * sizes[0] + 6 * width_in) * width_out,
                transcendentals=0,
            ),
        )(*blocks, held, *([] if total is None else [total]))

    (total,) = summed(NEAR, [near[key] for key in NEAR], after(context[0, 0], *back, far[1, 1, 0]), None, ())
    send(far, downward, (1, 1), (2, 1))
    for spot in ((0, 0), (0, 1), (-1, 0), (1, 0)):
        send(far, to_sibling, spot, spot, total, far_context)
    share(far, (-1, 1), (1, 1), (2, 0))
    total, late_context = summed(
        EARLY, [far[key] for key in EARLY], after(far_context, from_next, from_prior), total, LATE
    )
    send(far, to_sibling, (2, 1), (2, 1), total)
    late = len(LATE) * rows

    wide = 1024
    columns = pl.BlockSpec((width_in, wide), lambda i: (0, i))
    weight_grad = pl.pallas_call(
        last_kernel,
        out_shape=jax.ShapeDtypeStruct((width_in, width_out), jnp.bfloat16),
        grid=(width_out // wide,),
        in_specs=[pl.BlockSpec((rows, wide), lambda i: (0, i))] * len(LATE)
        + [pl.BlockSpec((width_in, late), lambda i: (0, 0)), columns],
        out_specs=columns,
        scratch_shapes=[pltpu.VMEM((late, wide), jnp.bfloat16)],
        compiler_params=pltpu.CompilerParams(vmem_limit_bytes=12 * 2**20),
        cost_estimate=pl.CostEstimate(
            flops=flops // 4, bytes_accessed=(2 * late + 6 * width_in) * width_out,
            transcendentals=0,
        ),
    )(*(far[key] for key in LATE), late_context, total)
    return (weight_grad[None], input_grad)


def solution(mesh):
    placed = (
        P("pipe", None, "tensor", None),
        P("pipe", None, None, "tensor"),
        P("pipe", None, "tensor", None),
    )
    return jax.shard_map(
        shards,
        mesh=mesh,
        in_specs=placed,
        out_specs=(P("pipe", "tensor", None), P("pipe", None, None, "tensor")),
        check_vma=False,
    )
```

```python
import functools

import jax
import jax.numpy as jnp
from jax import lax
from jax.experimental import pallas as pl
from jax.experimental.pallas import tpu as pltpu
from jax.sharding import PartitionSpec as P

RING = 4
PLANES = 2
CORES = 2
ANY = pl.BlockSpec(memory_space=pl.ANY)
VMEM = pl.BlockSpec(memory_space=pltpu.VMEM)
HBM = pl.BlockSpec(memory_space=pltpu.HBM)
NEAR = tuple((dy, dz, dc) for dz in range(PLANES) for dy in (0, -1, 1, 2) for dc in range(CORES))
LATE = tuple((2, dz, dc) for dz in range(PLANES) for dc in range(CORES))
EARLY = tuple(key for key in NEAR if key not in LATE)


def place(y, plane, core):
    return (y * PLANES + plane) * CORES + core


def moved(value, step):
    pairs = []
    for y in range(RING):
        for plane in range(PLANES):
            for core in range(CORES):
                pairs.append((place(y, plane, core), place(*step(y, plane, core))))
    return lax.ppermute(value, "tensor", pairs)


def upward(value):
    return moved(value, lambda y, plane, core: ((y + 1) % RING, plane, core))


def downward(value):
    return moved(value, lambda y, plane, core: ((y - 1) % RING, plane, core))


def across(value):
    return moved(value, lambda y, plane, core: (y, 1 - plane, core))


def to_sibling(value):
    return moved(value, lambda y, plane, core: (y, plane, 1 - core))


def mirrored(value):
    count = lax.axis_size("pipe")
    return lax.ppermute(value, "pipe", [(i, count - 1 - i) for i in range(count)])


def from_behind(value, by):
    count = lax.axis_size("pipe")
    pairs = [(i, i + by) for i in range(count) if 0 <= i + by < count]
    return lax.ppermute(value, "pipe", pairs)


def after(value, *earlier):
    return lax.optimization_barrier((value, *earlier))[0]


def first_row(key, rows):
    t = lax.axis_index("tensor")
    dy, dz, dc = key
    core = t % CORES
    plane = (t // CORES) % PLANES
    y = (t // (CORES * PLANES) + dy + RING) % RING
    block = place(y, 1 - plane if dz else plane, 1 - core if dc else core)
    return pl.multiple_of(block * rows, rows)


def run(copies):
    for copy in copies:
        copy.start()
    for copy in copies:
        copy.wait()


def back_kernel(*refs):
    n = len(NEAR)
    blocks = refs[:n]
    weights, first, second, whole, held, bsems, wsems = refs[n:]
    rows = blocks[0].shape[1]
    copies = [pltpu.make_async_copy(weights.at[r], held.at[r], wsems.at[r]) for r in range(2)]
    for i, key in enumerate(NEAR):
        target = whole.at[:, pl.ds(first_row(key, rows), rows), :]
        copies.append(pltpu.make_async_copy(blocks[i], target, bsems.at[i]))
    run(copies)
    tile = 384
    for r, out in enumerate((first, second)):
        for i in range(out.shape[0] // tile):
            span = slice(i * tile, (i + 1) * tile)
            out[span, :] = lax.dot_general(
                whole[r, span, :], held[r], (((1,), (1,)), ((), ())),
                preferred_element_type=jnp.float32,
            ).astype(out.dtype)


def sum_kernel(keys, late_keys, more, *refs):
    n = len(keys)
    blocks, context, rest = refs[:n], refs[n], refs[n + 1 :]
    if more:
        before, *rest = rest
    if late_keys:
        total, late, *rest = rest
    else:
        total, *rest = rest
    whole, upright, flat, bsems, csems = rest
    rows = whole.shape[0] // n
    copies, turned = [], []
    for i, block in enumerate(blocks):
        source = block.at[0] if len(block.shape) == 3 else block
        copies.append(
            pltpu.make_async_copy(source, whole.at[pl.ds(i * rows, rows), :], bsems.at[i])
        )
    for i, key in enumerate(keys + late_keys):
        source = context.at[pl.ds(first_row(key, rows), rows), :]
        target = upright.at[pl.ds(i * rows, rows), :]
        turned.append(pltpu.make_async_copy(source, target, csems.at[i]))
    for copy in turned + copies:
        copy.start()
    for copy in turned:
        copy.wait()
    count = n * rows
    flat[...] = upright[pl.ds(0, count), :].T
    if late_keys:
        late[...] = upright[pl.ds(count, len(late_keys) * rows), :].T
    for copy in copies:
        copy.wait()
    wide = 512

    @pl.loop(0, total.shape[1] // wide)
    def _(i):
        cols = pl.ds(pl.multiple_of(i * wide, wide), wide)
        product = jnp.dot(flat[...], whole[:, cols], preferred_element_type=jnp.float32)
        total[:, cols] = before[:, cols] + product if more else product


def last_kernel(*refs):
    n = len(LATE)
    context, total, out, whole = refs[n:]
    rows = refs[0].shape[0]
    for i, block in enumerate(refs[:n]):
        whole[pl.ds(i * rows, rows), :] = block[...]
    out[...] = (
        total[...] + jnp.dot(context[...], whole[...], preferred_element_type=jnp.float32)
    ).astype(out.dtype)


def shards(section_weights, context, grad_out):
    tokens, width_in = context.shape[2:]
    rows, width_out = grad_out.shape[2:]
    flops = 2 * tokens * width_in * width_out

    near = {(0, 0, 0): grad_out[0]}
    far = {}

    def send(held, move, begin, end, *earlier):
        key = (*end, int(move is to_sibling))
        held[key] = move(after(held[(*begin, 0)], *earlier))
        return held[key]

    def share(held, *spots):
        for spot in spots:
            held[(*spot, 1)] = to_sibling(held[(*spot, 0)])
        return [held[(*spot, 1)] for spot in spots]

    step = [
        send(near, upward, (0, 0), (-1, 0)),
        send(near, downward, (0, 0), (1, 0)),
        send(near, across, (0, 0), (0, 1)),
    ]
    far[0, 0, 0] = mirrored(after(grad_out[0, 1], *step))
    up_context = context[0, 1]
    step.append(up_context)
    step = [
        send(near, upward, (-1, 0), (2, 0), *step),
        send(near, downward, (0, 1), (1, 1), *step),
        far[0, 0, 0],
        *share(near, (0, 0), (-1, 0), (1, 0), (0, 1)),
    ]
    step = [
        send(near, upward, (0, 1), (-1, 1), *step),
        send(near, downward, (1, 1), (2, 1), *step),
        send(far, across, (0, 0), (0, 1), *step),
    ]
    for spot in ((2, 0), (1, 1)):
        send(near, to_sibling, spot, spot, far[0, 1, 0])
    for spot in ((-1, 1), (2, 1)):
        send(near, to_sibling, spot, spot, *step)
    send(far, upward, (0, 0), (-1, 0), *step)
    send(far, downward, (0, 0), (1, 0), *step)
    far_context = mirrored(after(up_context, *step))

    back_shape = jax.ShapeDtypeStruct((tokens, width_in), jnp.bfloat16)
    back = pl.pallas_call(
        back_kernel,
        out_shape=(back_shape,) * 2,
        in_specs=[HBM] + [ANY] * (len(NEAR) - 1) + [HBM],
        out_specs=(VMEM,) * 2,
        scratch_shapes=[
            pltpu.VMEM((2, tokens, width_out), jnp.bfloat16),
            pltpu.VMEM((2, width_in, width_out), jnp.bfloat16),
            pltpu.SemaphoreType.DMA((len(NEAR),)),
            pltpu.SemaphoreType.DMA((2,)),
        ],
        compiler_params=pltpu.CompilerParams(vmem_limit_bytes=40 * 2**20),
        cost_estimate=pl.CostEstimate(
            flops=2 * flops, bytes_accessed=4 * (tokens + width_in) * width_out, transcendentals=0
        ),
    )(*(near[key] for key in NEAR), section_weights[0])
    from_next = from_behind(back[0], -1)
    from_prior = from_behind(back[1], 1)
    input_grad = jnp.stack([from_next, from_prior])[None]

    send(far, upward, (0, 1), (-1, 1), back[0])
    send(far, downward, (0, 1), (1, 1), back[0])
    send(far, upward, (-1, 0), (2, 0), back[0])

    def summed(keys, blocks, held, total, late):
        count = len(keys)
        everything = keys + late
        sizes = count * rows, len(late) * rows
        shapes = [jax.ShapeDtypeStruct((width_in, width_out), jnp.float32)]
        if late:
            shapes.append(jax.ShapeDtypeStruct((width_in, sizes[1]), jnp.bfloat16))
        return pl.pallas_call(
            functools.partial(sum_kernel, keys, late, total is not None),
            out_shape=tuple(shapes),
            in_specs=[ANY] * count + [ANY] + [VMEM] * (total is not None),
            out_specs=(VMEM,) * len(shapes),
            scratch_shapes=[
                pltpu.VMEM((sizes[0], width_out), jnp.bfloat16),
                pltpu.VMEM((sum(sizes), width_in), jnp.bfloat16),
                pltpu.VMEM((width_in, sizes[0]), jnp.bfloat16),
                pltpu.SemaphoreType.DMA((count,)),
                pltpu.SemaphoreType.DMA((len(everything),)),
            ],
            compiler_params=pltpu.CompilerParams(vmem_limit_bytes=18 * 2**20),
            cost_estimate=pl.CostEstimate(
                flops=2 * sizes[0] * width_in * width_out,
                bytes_accessed=(2 * sizes[0] + 6 * width_in) * width_out,
                transcendentals=0,
            ),
        )(*blocks, held, *([] if total is None else [total]))

    (total,) = summed(NEAR, [near[key] for key in NEAR], after(context[0, 0], *back, far[1, 1, 0]), None, ())
    send(far, downward, (1, 1), (2, 1))
    for spot in ((0, 0), (0, 1), (-1, 0), (1, 0)):
        send(far, to_sibling, spot, spot, total, far_context)
    share(far, (-1, 1), (1, 1), (2, 0))
    total, late_context = summed(
        EARLY, [far[key] for key in EARLY], after(far_context, from_next, from_prior), total, LATE
    )
    send(far, to_sibling, (2, 1), (2, 1), total)
    late = len(LATE) * rows

    wide = 1024
    columns = pl.BlockSpec((width_in, wide), lambda i: (0, i))
    weight_grad = pl.pallas_call(
        last_kernel,
        out_shape=jax.ShapeDtypeStruct((width_in, width_out), jnp.bfloat16),
        grid=(width_out // wide,),
        in_specs=[pl.BlockSpec((rows, wide), lambda i: (0, i))] * len(LATE)
        + [pl.BlockSpec((width_in, late), lambda i: (0, 0)), columns],
        out_specs=columns,
        scratch_shapes=[pltpu.VMEM((late, wide), jnp.bfloat16)],
        compiler_params=pltpu.CompilerParams(vmem_limit_bytes=12 * 2**20),
        cost_estimate=pl.CostEstimate(
            flops=flops // 4, bytes_accessed=(2 * late + 6 * width_in) * width_out,
            transcendentals=0,
        ),
    )(*(far[key] for key in LATE), late_context, total)
    return (weight_grad[None], input_grad)


def solution(mesh):
    placed = (
        P("pipe", None, "tensor", None),
        P("pipe", None, None, "tensor"),
        P("pipe", None, "tensor", None),
    )
    return jax.shard_map(
        shards,
        mesh=mesh,
        in_specs=placed,
        out_specs=(P("pipe", "tensor", None), P("pipe", None, None, "tensor")),
        check_vma=False,
    )
```
